256 devices in a mesh: pb: 16 (over y_hi, x, core), ka: 16 (over y_lo, z).
Axes of the slice: x: 4, y: 4 (y_hi: 2, y_lo: 2; y = y_hi * 2 + y_lo), z: 8, core: 2. Of those that a mesh axis runs over, the one named last changes fastest.
Arguments:
- queries: bfloat16 [32768, 1024], P(('pb', 'ka')), may hold values from -200 to 200
- keys: bfloat16 [32768, 128], P(('pb', 'ka')), may hold values from -6 to 6
- values: bfloat16 [32768, 128], P(('pb', 'ka')), may hold values from -6 to 6
- positions: int32 [32768], replicated, may hold values from 0 to 32767, as said below
Outputs:
- attended: float32 [32768, 1024], P(('pb', 'ka'))
The draws below stay inside these ranges and needn't reach their ends.
Inputs may be any that keep to these rules, and one draw needn't show every extreme that they name: A permutation of 0 to 32767; each aligned run of 128 slots holds consecutive positions in increasing order.
All inputs are finite; a program needn't handle non-finite values.
Results may differ from the reference program's by a relative error of at most 0.0003.
Values may be sent and summed in bfloat16 or wider, within the bound.
A program may use at most 64 MiB of HBM per device.

```python
import jax
import jax.numpy as jnp
from jax import lax

HD = 128
H = 8
TOK_DEV = 128
SEQ = 32768


def joint_draw(key):
    base = jax.random.fold_in(key, 11)
    key_query, key_key, key_pos = jax.random.split(base, 3)
    runs = SEQ // TOK_DEV
    order = jax.random.permutation(key_pos, runs).astype(jnp.int32)
    positions = (order[:, None] * TOK_DEV + jnp.arange(TOK_DEV, dtype=jnp.int32)[None, :]).reshape(-1)
    keys = jnp.clip(jax.random.normal(key_key, (SEQ, HD), jnp.float32), -6.0, 6.0)
    queries = jnp.clip(jax.random.normal(key_query, (SEQ, H * HD), jnp.float32), -6.0, 6.0)
    return (queries, keys, positions)


def draw_queries(key, part):
    return joint_draw(key)[0].astype(jnp.bfloat16)


def draw_keys(key, part):
    return joint_draw(key)[1].astype(jnp.bfloat16)


def draw_positions(key, part):
    return joint_draw(key)[2]


def level_of(own_key, shape, cuts, least, high):
    gain = 1.0
    for dim, blocks in cuts:
        draws = jax.random.uniform(jax.random.fold_in(jax.random.fold_in(own_key, 6), dim), (blocks,), jnp.float32, least / len(cuts), high / len(cuts))
        gain = gain * jnp.repeat(jnp.exp(draws), shape[dim] // blocks).reshape((-1,) + (1,) * (len(shape) - 1 - dim))
    return gain


def centred(key, dims, deviation, limit, pieces=(), held_as=jnp.bfloat16):
    result = deviation * jax.random.normal(key, dims, jnp.float32)
    if pieces:
        result = result * level_of(key, dims, pieces, -0.22, 0.18)
    return jnp.clip(result, -limit, limit).astype(held_as)


def setup_inputs(seed: int = 0) -> dict:
    splits = jax.random.split(jax.random.key(seed), 5)
    return {
        "queries": draw_queries(jax.random.fold_in(splits[4], 71), 0),
        "keys": draw_keys(jax.random.fold_in(splits[4], 71), 0),
        "values": centred(splits[2], (SEQ, HD), 1.0, 6.0, ((0, 256),)),
        "positions": draw_positions(jax.random.fold_in(splits[4], 71), 0),
    }


def reference(queries, keys, values, positions):
    total_rows = queries.shape[0]
    block = min(128, total_rows)
    scale = 1.0 / (HD ** 0.5)
    keys_wide = keys.astype(jnp.float32)
    values_wide = values.astype(jnp.float32)

    def one_block(index):
        rows = lax.dynamic_slice_in_dim(queries, index * block, block, 0).astype(jnp.float32).reshape(block, H, HD)
        row_pos = lax.dynamic_slice_in_dim(positions, index * block, block, 0)
        score = jnp.einsum("qhd,kd->hqk", rows, keys_wide, precision=lax.Precision.HIGHEST) * scale
        visible = positions[None, None, :] <= row_pos[None, :, None]
        masked = jnp.where(visible, score, jnp.float32(-1e30))
        top = jnp.max(masked, axis=-1, keepdims=True)
        prob = jnp.where(visible, jnp.exp(masked - top), jnp.float32(0.0))
        total = jnp.sum(prob, axis=-1)
        output = jnp.einsum("hqk,kd->hqd", prob, values_wide, precision=lax.Precision.HIGHEST)
        output = output / total[:, :, None]
        return jnp.transpose(output, (1, 0, 2)).reshape(block, H * HD)

    blocks = lax.map(one_block, jnp.arange(total_rows // block, dtype=jnp.int32))
    return blocks.reshape(total_rows, H * HD)
```

```python
import functools

import jax
import jax.numpy as jnp
from jax import lax
from jax.experimental import pallas as pl
from jax.experimental.pallas import tpu as pltpu
from jax.sharding import Mesh
from jax.sharding import PartitionSpec as P

AXES = ("yh", "x", "c", "yl", "z")
NX, NC, NY, NZ = 4, 2, 4, 8
NH = NX * NC
HD = 128
RUN = 128
C = 1.4426950408889634 / HD**0.5
F32, BF16 = jnp.float32, jnp.bfloat16
GROUP, REACH = 4, 4
NT = (((1,), (1,)), ((), ()))
LOW, HIGH = 2.0**-60, 2.0**100
EMPTY = -1e30

def places(ranks):
    n = ranks.shape[0]
    place = jnp.sum((ranks[None, :] < ranks[:, None]).astype(jnp.int32), axis=1)
    hit = place[None, :] == jnp.arange(n, dtype=jnp.int32)[:, None]
    order = jnp.sum(jnp.where(hit, jnp.arange(n, dtype=jnp.int32)[None, :], 0), axis=1)
    held = jnp.sum(jnp.where(hit, ranks[None, :], 0), axis=1)
    return order, held

def plan(q_ranks, k_ranks, group, reach):
    q_order, q_held = places(q_ranks)
    k_order, k_held = places(k_ranks)
    seen = jnp.sum((k_ranks[None, :] <= q_held[:, None]).astype(jnp.int32), axis=1)
    tops = seen[group - 1 :: group]
    chunks = jnp.maximum((tops + reach - 1) // reach, 1)
    pad = jnp.zeros((group,), jnp.int32)
    return jnp.concatenate([
        q_order, pad, q_held, pad - 1, k_order, k_held, seen, pad, chunks, jnp.ones((1,), jnp.int32),
        jnp.sum(chunks)[None],
    ])

def attend(group, reach, n_q, n_k, meta, q_ref, k_ref, v_ref, out_ref, s0, s1, acc, sums):
    blocks = n_q // group
    o_q, o_qr = 0, n_q + group
    o_k = 2 * (n_q + group)
    o_kr = o_k + n_k
    o_seen = o_kr + n_k
    o_ch = o_seen + n_q + group
    o_tot = o_ch + blocks + 1
    diff = lax.broadcasted_iota(jnp.int32, (RUN, RUN), 1) - lax.broadcasted_iota(jnp.int32, (RUN, RUN), 0)

    def rows_q(b):
        return jnp.concatenate([q_ref[meta[o_q + b * group + g]] for g in range(group)], axis=0)

    def rows_k(ref, j):
        return jnp.concatenate([ref[meta[o_k + j * reach + r]] for r in range(reach)], axis=0)

    def scores(b, j, s_ref):
        s_ref[...] = lax.dot_general(rows_q(b), rows_k(k_ref, j), NT, preferred_element_type=F32)

    def weigh(b, j, s_ref):
        high, low, part = [], [], []
        for g in range(group):
            own = meta[o_qr + b * group + g]
            row_h, row_l, row_s = [], [], None
            for r in range(reach):
                gap = (own - meta[o_kr + j * reach + r]) * RUN
                s = s_ref[g * RUN : (g + 1) * RUN, r * RUN : (r + 1) * RUN]
                p = jnp.where(diff <= gap, jnp.exp2(s * C), 0.0)
                h = p.astype(BF16)
                row_h.append(h)
                row_l.append((p - h.astype(F32)).astype(BF16))
                row_s = p if row_s is None else row_s + p
            high.append(jnp.concatenate(row_h, axis=1))
            low.append(jnp.concatenate(row_l, axis=1))
            part.append(row_s)
        v = rows_k(v_ref, j)
        new = jnp.dot(jnp.concatenate(high, axis=0), v, preferred_element_type=F32)
        new += jnp.dot(jnp.concatenate(low, axis=0), v, preferred_element_type=F32)
        at = pl.ds(pl.multiple_of(b * group * RUN, RUN), group * RUN)
        first = j == 0
        acc[at, :] = jnp.where(first, 0.0, acc[at, :]) + new
        sums[at, :] = jnp.where(first, 0.0, sums[at, :]) + jnp.concatenate(part, axis=0)

    def after(b, j):
        b = jnp.minimum(b, blocks)
        last = j + 1 >= meta[o_ch + b]
        return jnp.minimum(jnp.where(last, b + 1, b), blocks), jnp.where(last, 0, j + 1)

    scores(0, 0, s0)

    def pair(_, at):
        b, j = at
        b1, j1 = after(b, j)
        scores(b1, j1, s1)
        weigh(b, j, s0)
        b2, j2 = after(b1, j1)
        scores(b2, j2, s0)
        weigh(b1, j1, s1)
        return b2, j2

    lax.fori_loop(0, (meta[o_tot] + 1) // 2, pair, (jnp.int32(0), jnp.int32(0)))

    def close(p, _):
        at = pl.ds(pl.multiple_of(p * RUN, RUN), RUN)
        slot = meta[o_q + p]
        seen = meta[o_seen + p]
        total = jnp.sum(sums[at, :].T, axis=0, keepdims=True)
        out_ref[slot, :RUN, :] = acc[at, :]
        peak = jnp.where(seen > 0, 0.0, EMPTY)
        out_ref[slot, RUN:, :] = jnp.concatenate([total, jnp.full((7, RUN), peak, F32)], axis=0)
        good = jnp.logical_and(total > LOW, total < HIGH)
        bad = jnp.sum(jnp.where(good, 0.0, 1.0)) > 0.0

        @pl.when(jnp.logical_and(bad, seen > 0))
        def _():
            q = q_ref[slot]
            own = meta[o_qr + p]

            def step(i, state):
                top, tot, got = state
                run = meta[o_k + i]
                gap = (own - meta[o_kr + i]) * RUN
                s = lax.dot_general(q, k_ref[run], NT, preferred_element_type=F32) * C
                keep = diff <= gap
                s = jnp.where(keep, s, EMPTY)
                new = jnp.maximum(top, jnp.max(s, axis=1, keepdims=True))
                w = jnp.where(keep, jnp.exp2(s - new), 0.0)
                f = jnp.exp2(top - new)
                h = w.astype(BF16)
                l = (w - h.astype(F32)).astype(BF16)
                v = v_ref[run]
                got = got * f + (jnp.dot(h, v, preferred_element_type=F32) + jnp.dot(l, v, preferred_element_type=F32))
                return new, tot * f + jnp.sum(w, axis=1, keepdims=True), got

            zero = jnp.zeros((RUN, 1), F32)
            top, tot, got = lax.fori_loop(0, seen, step, (zero + EMPTY, zero, jnp.zeros((RUN, HD), F32)))
            out_ref[slot, :RUN, :] = got
            wide = jnp.broadcast_to(tot, (RUN, RUN)).T
            peaks = jnp.broadcast_to(top, (RUN, RUN)).T
            out_ref[slot, RUN:, :] = jnp.concatenate([wide[:1], peaks[:7]], axis=0)

        return 0

    lax.fori_loop(0, n_q, close, 0)

def attend_call(meta, q, k, v, group, reach):
    n_q, n_k = q.shape[0], k.shape[0]
    vm = pl.BlockSpec(memory_space=pltpu.VMEM)
    return pl.pallas_call(
        functools.partial(attend, group, reach, n_q, n_k),
        out_shape=jax.ShapeDtypeStruct((n_q, RUN + 8, HD), F32),
        in_specs=[pl.BlockSpec(memory_space=pltpu.SMEM), vm, vm, vm],
        out_specs=vm,
        scratch_shapes=[
            pltpu.VMEM((group * RUN, reach * RUN), F32),
            pltpu.VMEM((group * RUN, reach * RUN), F32),
            pltpu.VMEM(((n_q + group) * RUN, HD), F32),
            pltpu.VMEM(((n_q + group) * RUN, RUN), F32),
        ],
        compiler_params=pltpu.CompilerParams(vmem_limit_bytes=50 << 20),
        name="attend",
    )(meta, q, k, v)


def here():
    y = lax.axis_index("yh") * 2 + lax.axis_index("yl")
    return lax.axis_index("x"), lax.axis_index("c"), y, lax.axis_index("z")


def device(x, c, y, z):
    return {"yh": y // 2, "x": x, "c": c, "yl": y % 2, "z": z}


def remote(src, dst, send_sem, recv_sem, target):
    return pltpu.make_async_remote_copy(
        src_ref=src, dst_ref=dst, send_sem=send_sem, recv_sem=recv_sem,
        device_id=device(*target), device_id_type=pl.DeviceIdType.MESH,
    )


def near_first(t, n):
    odd = t % 2
    return odd * ((t + 1) // 2) + (1 - odd) * ((n - t // 2) % n)


def spread(q_ref, k_ref, v_ref, qo, ko, vo, q_in, k_in, l_in, u_in, c_in, q_s1, q_s2, k_s1, k_s2, l_s1, l_s2, u_s1, u_s2, c_out):
    x, c, y, z = here()
    lane = x * NC + c
    half = RUN // 2
    low, up = pl.ds(0, half), pl.ds(half, half)

    barrier = pltpu.get_barrier_semaphore()
    for d in range(1, NZ):
        pl.semaphore_signal(barrier, 1, device_id=device(x, c, y, (z + d) % NZ), device_id_type=pl.DeviceIdType.MESH)
    for d in range(1, NH):
        to = (lane + d) % NH
        pl.semaphore_signal(barrier, 1, device_id=device(to // NC, to % NC, y, z), device_id_type=pl.DeviceIdType.MESH)
    for d in range(1, NY):
        pl.semaphore_signal(barrier, 1, device_id=device(x, c, (y + d) % NY, z), device_id_type=pl.DeviceIdType.MESH)
    pl.semaphore_wait(barrier, NZ + NH + NY - 3)

    def slot(xx, zz):
        return (xx * NC + c) * NZ + zz

    def q_cols(h):
        return q_ref.at[:, pl.ds(pl.multiple_of(h * HD, HD), HD)]

    own_q = qo.at[y * NH + lane]
    mine = slot(x, z)

    def k_first(d):
        return remote(k_ref, ko.at[mine], k_s1.at[d], k_in.at[x, z], (x, c, y, (z + d) % NZ))

    def l_first(d):
        return remote(v_ref.at[low, :], vo.at[mine, low, :], l_s1.at[d], l_in.at[x, z], (x, c, y, (z + d) % NZ))

    def u_first(d):
        return remote(v_ref.at[up, :], vo.at[mine, up, :], u_s1.at[d], u_in.at[x, z], ((x + d) % NX, c, y, z))

    def q_first(d):
        to = (lane + d) % NH
        return remote(q_cols(to), own_q, q_s1.at[d], q_in.at[y, lane], (to // NC, to % NC, y, z))

    for d in (1, 3, 2):
        u_first(d).start()
    for d in range(1, NH):
        q_first(d).start()
    for d in (1, 7, 2, 6, 3, 5, 4):
        k_first(d).start()
        l_first(d).start()
    pltpu.make_async_copy(k_ref, ko.at[mine], k_in.at[x, z]).start()
    pltpu.make_async_copy(v_ref.at[low, :], vo.at[mine, low, :], l_in.at[x, z]).start()
    pltpu.make_async_copy(v_ref.at[up, :], vo.at[mine, up, :], u_in.at[x, z]).start()
    pltpu.make_async_copy(q_cols(lane), own_q, q_in.at[y, lane]).start()

    def k_next(zz, d):
        s = slot(x, zz)
        return remote(ko.at[s], ko.at[s], k_s2.at[d, zz], k_in.at[x, zz], ((x + d) % NX, c, y, z))

    def l_next(zz, d):
        s = slot(x, zz)
        return remote(vo.at[s, low, :], vo.at[s, low, :], l_s2.at[d, zz], l_in.at[x, zz], ((x + d) % NX, c, y, z))

    def u_next(xx, d):
        s = slot(xx, z)
        return remote(vo.at[s, up, :], vo.at[s, up, :], u_s2.at[d, xx], u_in.at[xx, z], (x, c, y, (z + d) % NZ))

    def q_next(h, d):
        s = y * NH + h
        return remote(qo.at[s], qo.at[s], q_s2.at[d, h], q_in.at[y, h], (x, c, (y + d) % NY, z))

    def got_k(xx, zz):
        s = slot(xx, zz)
        pltpu.make_async_copy(ko.at[s], ko.at[s], k_in.at[xx, zz]).wait()
        pltpu.make_async_copy(vo.at[s, low, :], vo.at[s, low, :], l_in.at[xx, zz]).wait()

    def got_u(xx, zz):
        s = slot(xx, zz)
        pltpu.make_async_copy(vo.at[s, up, :], vo.at[s, up, :], u_in.at[xx, zz]).wait()

    def got_q(yy, h):
        s = yy * NH + h
        pltpu.make_async_copy(qo.at[s], qo.at[s], q_in.at[yy, h]).wait()

    def relay(t, _):
        zz = (z + near_first(t, NZ)) % NZ
        got_k(x, zz)
        for d in (1, 3, 2):
            k_next(zz, d).start()
            l_next(zz, d).start()
        h = (lane + near_first(t, NH)) % NH
        got_q(y, h)
        for d in (1, 3, 2):
            q_next(h, d).start()
        return 0

    def relay_up(t, _):
        xx = (x + near_first(t, NX)) % NX
        got_u(xx, z)
        for d in (1, 7, 2, 6, 3, 5, 4):
            u_next(xx, d).start()
        return 0

    lax.fori_loop(0, 3, relay, 0)
    lax.fori_loop(0, NX, relay_up, 0)
    lax.fori_loop(3, NZ, relay, 0)

    def share(xx, half_of, ref):
        part = pl.ds(pl.multiple_of(slot(xx, 0), NZ), NZ)
        return remote(ref.at[part], ref.at[part], c_out.at[half_of, xx], c_in.at[half_of, xx], (x, 1 - c, y, z))

    def pass_on(t, _):
        xx = (x + near_first(t, NX)) % NX

        @pl.when(t > 0)
        def _():
            lax.fori_loop(0, NZ, lambda i, _: (got_k(xx, i), 0)[1], 0)

        lax.fori_loop(1, NZ, lambda i, _: (got_u(xx, (z + i) % NZ), 0)[1], 0)
        share(xx, 0, ko).start()
        share(xx, 1, vo).start()
        return 0

    lax.fori_loop(0, NX, pass_on, 0)

    def all_q(t, _):
        lax.fori_loop(0, NH, lambda h, _: (got_q((y + t) % NY, h), 0)[1], 0)
        return 0

    lax.fori_loop(1, NY, all_q, 0)

    def shared(xx, _):
        share(xx, 0, ko).wait_send()
        share(xx, 1, vo).wait_send()
        other = pl.ds(pl.multiple_of((xx * NC + 1 - c) * NZ, NZ), NZ)
        pltpu.make_async_copy(ko.at[other], ko.at[other], c_in.at[0, xx]).wait()
        pltpu.make_async_copy(vo.at[other], vo.at[other], c_in.at[1, xx]).wait()
        return 0

    lax.fori_loop(0, NX, shared, 0)

    for d in range(1, NX):
        u_first(d).wait_send()
    for d in range(1, NH):
        q_first(d).wait_send()
    for d in range(1, NZ):
        k_first(d).wait_send()
        l_first(d).wait_send()

    def sent(i, _):
        for d in range(1, NX):
            k_next(i, d).wait_send()
            l_next(i, d).wait_send()
            q_next(i, d).wait_send()
        return 0

    lax.fori_loop(0, NZ, sent, 0)

    def sent_up(i, _):
        for d in range(1, NZ):
            u_next(i, d).wait_send()
        return 0

    lax.fori_loop(0, NX, sent_up, 0)


def spread_call(q, k, v):
    vm = pl.BlockSpec(memory_space=pltpu.VMEM)
    anywhere = pl.BlockSpec(memory_space=pl.ANY)
    dma = pltpu.SemaphoreType.DMA
    return pl.pallas_call(
        spread,
        out_shape=(
            jax.ShapeDtypeStruct((NY * NH, RUN, HD), BF16),
            jax.ShapeDtypeStruct((NH * NZ, RUN, HD), BF16),
            jax.ShapeDtypeStruct((NH * NZ, RUN, HD), BF16),
        ),
        in_specs=[anywhere] * 3,
        out_specs=(vm, vm, vm),
        scratch_shapes=[
            dma((NY, NH)), dma((NX, NZ)), dma((NX, NZ)), dma((NX, NZ)), dma((2, NX)),
            dma((NH,)), dma((NY, NH)), dma((NZ,)), dma((NX, NZ)), dma((NZ,)), dma((NX, NZ)),
            dma((NX,)), dma((NZ, NX)), dma((2, NX)),
        ],
        compiler_params=pltpu.CompilerParams(collective_id=1, has_side_effects=True, vmem_limit_bytes=24 << 20),
        name="spread",
    )(q, k, v)


def gather_parts(p_ref, o_ref, got, send_sem, recv_sem):
    x, c, y, z = here()
    n = NY * NH
    me = y * NH + x * NC + c

    def target(t):
        to = (me + t) % n
        return to, (to // NC % NX, to % NC, to // NH, z)

    barrier = pltpu.get_barrier_semaphore()

    def greet(t, _):
        pl.semaphore_signal(barrier, 1, device_id=device(*target(t)[1]), device_id_type=pl.DeviceIdType.MESH)
        return 0

    lax.fori_loop(1, n, greet, 0)
    pl.semaphore_wait(barrier, n - 1)

    def part(t):
        to, where = target(t)
        return remote(p_ref.at[to], got.at[me], send_sem.at[t], recv_sem.at[me], where)

    lax.fori_loop(1, n, lambda t, _: (part(t).start(), 0)[1], 0)
    pltpu.make_async_copy(p_ref.at[me], got.at[me], recv_sem.at[me]).start()
    lax.fori_loop(0, n, lambda i, _: (pltpu.make_async_copy(got.at[i], got.at[i], recv_sem.at[i]).wait(), 0)[1], 0)

    rows = []
    for h in range(NH):
        totals = [got[s * NH + h, RUN : RUN + 1, :] for s in range(NY)]
        tops = [got[s * NH + h, RUN + 1 : RUN + 2, :] for s in range(NY)]
        top = functools.reduce(jnp.maximum, tops)
        factors = [jnp.exp2(t - top) for t in tops]
        whole = functools.reduce(jnp.add, [f * t for f, t in zip(factors, totals)])
        rows += [f / whole for f in factors]
    weights = jnp.concatenate(rows + [jnp.zeros((RUN - n, RUN), F32)], axis=0).T
    for h in range(NH):
        o_ref[:, h * HD : (h + 1) * HD] = functools.reduce(
            jnp.add, [got[s * NH + h, :RUN, :] * weights[:, h * NY + s : h * NY + s + 1] for s in range(NY)]
        )

    lax.fori_loop(1, n, lambda t, _: (part(t).wait_send(), 0)[1], 0)


def gather_call(parts):
    n = NY * NH
    return pl.pallas_call(
        gather_parts,
        out_shape=jax.ShapeDtypeStruct((RUN, NH * HD), F32),
        in_specs=[pl.BlockSpec(memory_space=pl.ANY)],
        out_specs=pl.BlockSpec(memory_space=pltpu.VMEM),
        scratch_shapes=[
            pltpu.VMEM((n, RUN + 8, HD), F32), pltpu.SemaphoreType.DMA((n,)), pltpu.SemaphoreType.DMA((n,)),
        ],
        compiler_params=pltpu.CompilerParams(collective_id=2, has_side_effects=True, vmem_limit_bytes=16 << 20),
        name="gather_parts",
    )(parts)


def on_device(queries, keys, values, positions):
    ranks = (positions.reshape(-1, RUN)[:, 0] // RUN).reshape(2, NX, NC, 2, NZ)
    yh, yl, z = lax.axis_index("yh"), lax.axis_index("yl"), lax.axis_index("z")
    q_ranks = lax.dynamic_index_in_dim(ranks, z, 4, False).transpose(0, 3, 1, 2).reshape(-1)
    k_ranks = lax.dynamic_index_in_dim(lax.dynamic_index_in_dim(ranks, yh, 0, False), yl, 2, False).reshape(-1)
    meta = plan(q_ranks, k_ranks, GROUP, REACH)
    q, k, v = spread_call(queries, keys, values)
    return gather_call(attend_call(meta, q, k, v, GROUP, REACH))


def solution(mesh):
    finer = Mesh(mesh.devices.reshape(2, NX, NC, 2, NZ), AXES)
    placed = (P(AXES, None), P(AXES, None), P(AXES, None), P())
    return jax.shard_map(on_device, mesh=finer, in_specs=placed, out_specs=P(AXES, None), check_vma=False)
```

```python
import functools

import jax
import jax.numpy as jnp
from jax import lax
from jax.experimental import pallas as pl
from jax.experimental.pallas import tpu as pltpu
from jax.sharding import Mesh
from jax.sharding import PartitionSpec as P

AXES = ("yh", "x", "c", "yl", "z")
NX, NC, NY, NZ = 4, 2, 4, 8
NH = NX * NC
HD = 128
RUN = 128
C = 1.4426950408889634 / HD**0.5
F32, BF16 = jnp.float32, jnp.bfloat16
GROUP, REACH = 4, 8
NT = (((1,), (1,)), ((), ()))
LOW, HIGH = 2.0**-60, 2.0**100
EMPTY = -1e30
STEPS, TINY = 32767.0, 2.0**-110

def plan(pos_ref, meta, n_q):
    x, c, y, z = here()
    n = pos_ref.shape[0]
    first = pos_ref[...].astype(F32) * (1.0 / RUN)
    column = first[:, :1]
    row = jnp.concatenate([first[i : i + RUN].T[:1] for i in range(0, n, RUN)], axis=1)

    def coords(axis, shape):
        i = lax.broadcasted_iota(jnp.int32, shape, axis)
        iz, iyl, ic, ix, iyh = i % NZ, i // NZ % 2, i // (2 * NZ) % NC, i // (2 * NZ * NC) % NX, i // (2 * NZ * NC * NX)
        iy = 2 * iyh + iyl
        return iz == z, iy == y, iy * NH + ix * NC + ic, (ix * NC + ic) * NZ + iz

    q_row, k_row, _, _ = coords(1, (1, n))
    q_col, k_col, q_slot, k_slot = coords(0, (n, 1))
    below = row < column

    def count(mask):
        return jnp.sum(jnp.where(mask, 1.0, 0.0), axis=1, keepdims=True)

    spot = lax.broadcasted_iota(jnp.int32, (1, RUN), 1).astype(F32)

    def sorted_by_rank(here_col, here_row, things):
        place = count(jnp.logical_and(below, here_row))
        hit = jnp.logical_and(place == spot, here_col)
        return [jnp.sum(jnp.where(hit, thing, 0.0), axis=0, keepdims=True) for thing in things]

    seen = count(jnp.logical_and(row <= column, k_row))
    order, held, sees = sorted_by_rank(q_col, q_row, (q_slot.astype(F32), column, seen))
    held = jnp.where(spot < n_q, held, -1.0)
    rows = [order, held, sees] + sorted_by_rank(k_col, k_row, (k_slot.astype(F32), column))
    meta[...] = jnp.concatenate(rows + [jnp.zeros((3, RUN), F32)], axis=0).astype(jnp.int32)


def attend(group, reach, n_q, n_k, pos_ref, q_ref, k_ref, v_ref, out_ref, stat_ref, s0, s1, acc, sums, found, meta, sem):
    blocks = n_q // group
    plan(pos_ref, found, n_q)
    copy = pltpu.make_async_copy(found, meta, sem)
    copy.start()
    copy.wait()

    def chunks(b):
        top = meta[2, jnp.minimum(b * group + group - 1, n_q - 1)]
        return jnp.where(b < blocks, jnp.maximum((top + reach - 1) // reach, 1), 1)

    diff = lax.broadcasted_iota(jnp.int32, (RUN, RUN), 1) - lax.broadcasted_iota(jnp.int32, (RUN, RUN), 0)

    def rows_q(b):
        return jnp.concatenate([q_ref[meta[0, b * group + g]] for g in range(group)], axis=0)

    def rows_k(ref, j):
        return jnp.concatenate([ref[meta[3, j * reach + r]] for r in range(reach)], axis=0)

    def scores(b, j, s_ref):
        s_ref[...] = lax.dot_general(rows_q(b), rows_k(k_ref, j), NT, preferred_element_type=F32)

    def weigh(b, j, s_ref):
        both, part = [], []
        for g in range(group):
            own = meta[1, b * group + g]
            row_h, row_l, row_s = [], [], None
            for r in range(reach):
                gap = (own - meta[4, j * reach + r]) * RUN
                s = s_ref[g * RUN : (g + 1) * RUN, r * RUN : (r + 1) * RUN]
                p = jnp.where(diff <= gap, jnp.exp2(s * C), 0.0)
                h = p.astype(BF16)
                row_h.append(h)
                row_l.append((p - h.astype(F32)).astype(BF16))
                row_s = p if row_s is None else row_s + p
            both.append(jnp.concatenate([x for pair in zip(row_h, row_l) for x in pair], axis=1))
            part.append(row_s)
        twice = jnp.concatenate([v_ref[meta[3, j * reach + r]] for r in range(reach) for _ in range(2)], axis=0)
        new = jnp.dot(jnp.concatenate(both, axis=0), twice, preferred_element_type=F32)
        at = pl.ds(pl.multiple_of(b * group * RUN, RUN), group * RUN)
        first = j == 0
        acc[at, :] = jnp.where(first, 0.0, acc[at, :]) + new
        sums[at, :] = jnp.where(first, 0.0, sums[at, :]) + jnp.concatenate(part, axis=0)

    def after(b, j):
        b = jnp.minimum(b, blocks)
        last = j + 1 >= chunks(b)
        return jnp.minimum(jnp.where(last, b + 1, b), blocks), jnp.where(last, 0, j + 1)

    total_chunks = functools.reduce(jnp.add, [chunks(b) for b in range(blocks)])
    scores(0, 0, s0)

    def pair(_, at):
        b, j = at
        b1, j1 = after(b, j)
        weigh(b, j, s0)
        scores(b1, j1, s1)
        b2, j2 = after(b1, j1)
        weigh(b1, j1, s1)
        scores(b2, j2, s0)
        return b2, j2

    lax.fori_loop(0, (total_chunks + 1) // 2, pair, (jnp.int32(0), jnp.int32(0)))

    lanes = lax.broadcasted_iota(jnp.int32, (RUN, RUN), 1)

    def coded(got, total):
        mean = got * jnp.where(total > 0.0, 1.0 / total, 0.0)
        reach_of = jnp.maximum(jnp.max(jnp.abs(mean), axis=1, keepdims=True), TINY)
        return jnp.round(mean * (STEPS / reach_of)).astype(jnp.int32).astype(jnp.int16), reach_of

    def close(p, table):
        at = pl.ds(pl.multiple_of(p * RUN, RUN), RUN)
        total = jnp.sum(sums[at, :], axis=1, keepdims=True)
        out_ref[meta[0, p]], widest = coded(acc[at, :], total)
        return jnp.where(lanes == 2 * p, total, jnp.where(lanes == 2 * p + 1, widest, table))

    table = lax.fori_loop(0, n_q, close, jnp.zeros((RUN, RUN), F32), unroll=4).T
    outside = jnp.zeros((1, RUN), F32)
    for p in range(n_q):
        seen = meta[2, p] > 0
        total = table[2 * p : 2 * p + 1]
        good = jnp.logical_and(total > LOW, total < HIGH)
        outside += jnp.where(good, 0.0, jnp.where(seen, 1.0, 0.0))
        peak = jnp.full((6, RUN), jnp.where(seen, 0.0, EMPTY), F32)
        stat_ref[meta[0, p]] = jnp.concatenate([table[2 * p : 2 * p + 2], peak], axis=0)

    @pl.when(jnp.sum(outside) > 0.0)
    def _():
        def again(p, _):
            slot = meta[0, p]
            q = q_ref[slot]
            own = meta[1, p]

            def step(i, state):
                top, tot, got = state
                run = meta[3, i]
                gap = (own - meta[4, i]) * RUN
                s = lax.dot_general(q, k_ref[run], NT, preferred_element_type=F32) * C
                keep = diff <= gap
                s = jnp.where(keep, s, EMPTY)
                new = jnp.maximum(top, jnp.max(s, axis=1, keepdims=True))
                w = jnp.where(keep, jnp.exp2(s - new), 0.0)
                f = jnp.exp2(top - new)
                h = w.astype(BF16)
                l = (w - h.astype(F32)).astype(BF16)
                v = v_ref[run]
                got = got * f + (jnp.dot(h, v, preferred_element_type=F32) + jnp.dot(l, v, preferred_element_type=F32))
                return new, tot * f + jnp.sum(w, axis=1, keepdims=True), got

            zero = jnp.zeros((RUN, 1), F32)
            top, tot, got = lax.fori_loop(0, meta[2, p], step, (zero + EMPTY, zero, jnp.zeros((RUN, HD), F32)))
            out_ref[slot], widest = coded(got, tot)
            stat_ref[slot] = jnp.where(lanes == 0, tot, jnp.where(lanes == 1, widest, top)).T[:8]
            return 0

        lax.fori_loop(0, n_q, again, 0)


def attend_call(first, q, k, v, group, reach):
    n_q, n_k = q.shape[0], k.shape[0]
    vm = pl.BlockSpec(memory_space=pltpu.VMEM)
    return pl.pallas_call(
        functools.partial(attend, group, reach, n_q, n_k),
        out_shape=(
            jax.ShapeDtypeStruct((n_q, RUN, HD), jnp.int16),
            jax.ShapeDtypeStruct((n_q, 8, RUN), F32),
        ),
        in_specs=[vm, vm, vm, vm],
        out_specs=(vm, vm),
        scratch_shapes=[
            pltpu.VMEM((group * RUN, reach * RUN), F32),
            pltpu.VMEM((group * RUN, reach * RUN), F32),
            pltpu.VMEM(((n_q + group) * RUN, HD), F32),
            pltpu.VMEM(((n_q + group) * RUN, RUN), F32),
            pltpu.VMEM((8, RUN), jnp.int32),
            pltpu.SMEM((8, RUN), jnp.int32),
            pltpu.SemaphoreType.DMA,
        ],
        compiler_params=pltpu.CompilerParams(vmem_limit_bytes=20 << 20),
        name="attend",
    )(first, q, k, v)


def here():
    y = lax.axis_index("yh") * 2 + lax.axis_index("yl")
    return lax.axis_index("x"), lax.axis_index("c"), y, lax.axis_index("z")


def device(x, c, y, z):
    return {"yh": y // 2, "x": x, "c": c, "yl": y % 2, "z": z}


def remote(src, dst, send_sem, recv_sem, target):
    return pltpu.make_async_remote_copy(
        src_ref=src, dst_ref=dst, send_sem=send_sem, recv_sem=recv_sem,
        device_id=device(*target), device_id_type=pl.DeviceIdType.MESH,
    )


def spread(q_ref, k_ref, v_ref, qo, ko, vo, q_in, k_in, v_in, kc_in, vc_in, q_near, q_far, k_z, k_x, v_x, v_z, k_c, v_c):
    x, c, y, z = here()
    lane = x * NC + c

    barrier = pltpu.get_barrier_semaphore()

    def greet(*where):
        pl.semaphore_signal(barrier, 1, device_id=device(*where), device_id_type=pl.DeviceIdType.MESH)

    for d in range(1, NZ):
        greet(x, c, y, (z + d) % NZ)
    for d in range(1, NH):
        to = (lane + d) % NH
        greet(to // NC, to % NC, y, z)
    for d in range(1, NY):
        greet(x, c, (y + d) % NY, z)
    pl.semaphore_wait(barrier, NZ + NH + NY - 3)

    def go(copy):
        copy.start()

    def at_x(d):
        return (x + d) % NX

    def at_z(d):
        return (z + d) % NZ

    def slot(dx, dz):
        return (at_x(dx) * NC + c) * NZ + at_z(dz)

    def k_to_x(dz, d):
        s = slot(0, dz)
        go(remote(ko.at[s], ko.at[s], k_x, k_in.at[x, at_z(dz)], (at_x(d), c, y, z)))

    def v_to_z(dx, dz, d):
        s = slot(dx, dz)
        go(remote(vo.at[s], vo.at[s], v_z, v_in.at[at_x(dx), at_z(dz)], (x, c, y, at_z(d))))

    def share(dx, dz, ref, out, into):
        s = slot(dx, dz)
        go(remote(ref.at[s], ref.at[s], out, into, (x, 1 - c, y, z)))

    def got(ref, s, sem):
        pltpu.make_async_copy(ref.at[s], ref.at[s], sem).wait()

    def got_k(dx, dz):
        got(ko, slot(dx, dz), k_in.at[at_x(dx), at_z(dz)])

    def got_v(dx, dz):
        got(vo, slot(dx, dz), v_in.at[at_x(dx), at_z(dz)])

    def got_q(d, h):
        yy = (y + d) % NY
        got(qo, yy * NH + h, q_in.at[yy, h])

    def q_cols(h):
        return q_ref.at[:, pl.ds(pl.multiple_of(h * HD, HD), HD)]

    own_q, own = qo.at[y * NH + lane], slot(0, 0)
    for d in (1, 3, 2):
        go(remote(v_ref, vo.at[own], v_x, v_in.at[x, z], (at_x(d), c, y, z)))
    for d in (1, NZ - 1, 2, NZ - 2, 3, NZ - 3, 4):
        go(remote(k_ref, ko.at[own], k_z, k_in.at[x, z], (x, c, y, at_z(d))))
    for d in range(1, NH):
        to = (lane + d) % NH
        go(remote(q_cols(to), own_q, q_near, q_in.at[y, lane], (to // NC, to % NC, y, z)))
    pltpu.make_async_copy(k_ref, ko.at[own], k_in.at[x, z]).start()
    pltpu.make_async_copy(v_ref, vo.at[own], v_in.at[x, z]).start()
    pltpu.make_async_copy(q_cols(lane), own_q, q_in.at[y, lane]).start()

    def side(t):
        d = (t + 1) // 2
        return d if t % 2 else -d

    def k_step(t):
        got_k(0, side(t))
        for d in (1, 3, 2):
            k_to_x(side(t), d)
        share(0, side(t), ko, k_c, kc_in)

    def k_rest(t):
        for dx in (1, -1, 2):
            got_k(dx, side(t))
            share(dx, side(t), ko, k_c, kc_in)

    def v_start(dx):
        got_v(dx, 0)
        v_to_z(dx, 0, 1)
        v_to_z(dx, 0, -1)
        share(dx, 0, vo, v_c, vc_in)

    def v_step(t):
        dz = side(t)
        for dx in (0, 1, -1, 2):
            got_v(dx, dz)
            if 0 < dz < NZ // 2:
                v_to_z(dx, dz, -1)
            elif 1 - NZ // 2 < dz < 0:
                v_to_z(dx, dz, 1)
            share(dx, dz, vo, v_c, vc_in)

    def q_step(t):
        h = (lane + t) % NH
        s = y * NH + h
        got_q(0, h)
        for d in (1, 3, 2):
            go(remote(qo.at[s], qo.at[s], q_far, q_in.at[y, h], (x, c, (y + d) % NY, z)))

    def near(t):
        k_step(t)
        q_step(t)

    v_start(0)
    near(0)
    for dx in (1, -1, 2):
        v_start(dx)
    near(1)
    near(2)
    v_step(1)
    v_step(2)
    for t in (3, 4, 5):
        near(t)
    v_step(3)
    v_step(4)
    near(6)
    near(7)
    for t in (0, 1, 2):
        k_rest(t)
    v_step(5)
    v_step(6)
    for t in (3, 4, 5):
        k_rest(t)
    v_step(7)
    k_rest(6)
    k_rest(7)

    def q_rest(i, _):
        got_q(1 + i // NH, i % NH)
        return 0

    lax.fori_loop(0, (NY - 1) * NH, q_rest, 0)
    for sem, count in (
        (kc_in, 32), (vc_in, 32), (q_near, 7), (q_far, 24), (k_z, 7), (k_x, 24), (v_x, 3), (v_z, 28), (k_c, 32), (v_c, 32),
    ):
        some = pl.ds(0, count)
        got(ko, some, sem)


def spread_call(q, k, v):
    vm = pl.BlockSpec(memory_space=pltpu.VMEM)
    held = pl.BlockSpec(memory_space=pltpu.HBM)
    dma = pltpu.SemaphoreType.DMA
    grid = (NX, NZ)
    return pl.pallas_call(
        spread,
        out_shape=(
            jax.ShapeDtypeStruct((NY * NH, RUN, HD), BF16),
            jax.ShapeDtypeStruct((NH * NZ, RUN, HD), BF16),
            jax.ShapeDtypeStruct((NH * NZ, RUN, HD), BF16),
        ),
        in_specs=[held] * 3,
        out_specs=(vm, vm, vm),
        scratch_shapes=[
            dma((NY, NH)), dma(grid), dma(grid), dma, dma, dma, dma, dma, dma, dma, dma, dma, dma,
        ],
        compiler_params=pltpu.CompilerParams(collective_id=1, has_side_effects=True, vmem_limit_bytes=8 << 20),
        name="spread",
    )(q, k, v)


def gather_parts(p_ref, t_ref, o_ref, got, stat, merged, far, near_in, p_in, t_in, p_out, t_out):
    x, c, y, z = here()
    lane = x * NC + c
    mine = pl.ds(pl.multiple_of(lane * HD, HD), HD)

    barrier = pltpu.get_barrier_semaphore()

    def greet(*where):
        pl.semaphore_signal(barrier, 1, device_id=device(*where), device_id_type=pl.DeviceIdType.MESH)

    for d in range(1, NY):
        greet(x, c, (y + d) % NY, z)
    for d in range(1, NH):
        to = (lane + d) % NH
        greet(to // NC, to % NC, y, z)
    pl.semaphore_wait(barrier, NY + NH - 2)

    order = (1, 3, 2, 0)
    for dx in order:
        xx = (x + dx) % NX
        for d in (1, 3, 2):
            yy = (y + d) % NY
            here_ = pl.ds(yy * NH + xx * NC, NC)
            lands = pl.ds(xx * NC, NC)
            remote(p_ref.at[here_], got.at[NY - d, lands], p_out, p_in.at[NY - d, xx], (x, c, yy, z)).start()
            remote(t_ref.at[here_], stat.at[NY - d, lands], t_out, t_in.at[NY - d, xx], (x, c, yy, z)).start()

    for dx in order:
        xx = (x + dx) % NX
        lands = pl.ds(xx * NC, NC)
        for d in (1, 3, 2):
            pltpu.make_async_copy(got.at[d, lands], got.at[d, lands], p_in.at[d, xx]).wait()
            pltpu.make_async_copy(stat.at[d, lands], stat.at[d, lands], t_in.at[d, xx]).wait()
        rows = []
        for cc in range(NC):
            to = xx * NC + cc
            stats = [t_ref[y * NH + to]] + [stat[d, to] for d in range(1, NY)]
            top = functools.reduce(jnp.maximum, [s[2:3] for s in stats])
            shares = [jnp.exp2(s[2:3] - top) * s[0:1] for s in stats]
            whole = functools.reduce(jnp.add, shares)
            rows += [f / whole * (s[1:2] * (1.0 / STEPS)) for f, s in zip(shares, stats)]
        weights = jnp.concatenate(rows + [jnp.zeros((RUN - NC * NY, RUN), F32)], axis=0).T
        for cc in range(NC):
            to = xx * NC + cc
            parts = [p_ref[y * NH + to]] + [got[d, to] for d in range(1, NY)]
            merged[to] = functools.reduce(
                jnp.add,
                [p.astype(jnp.int32).astype(F32) * weights[:, cc * NY + i : cc * NY + i + 1] for i, p in enumerate(parts)],
            )

            def send(to=to, cc=cc):
                remote(merged.at[to], o_ref.at[:, mine], far, near_in.at[lane], (xx, cc, y, z)).start()

            if dx:
                send()
            else:
                pl.when(c != cc)(send)

    o_ref[:, mine] = merged[lane]

    def landed(i, _):
        h = (lane + i) % NH
        cols = o_ref.at[:, pl.ds(pl.multiple_of(h * HD, HD), HD)]
        pltpu.make_async_copy(cols, cols, near_in.at[h]).wait()
        return 0

    lax.fori_loop(1, NH, landed, 0)
    sent = merged.at[pl.ds(0, NH - 1)]
    pltpu.make_async_copy(sent, sent, far).wait()
    for ref, sem in ((p_ref, p_out), (t_ref, t_out)):
        sent = ref.at[pl.ds(0, (NY - 1) * NH)]
        pltpu.make_async_copy(sent, sent, sem).wait()


def gather_call(parts, stats):
    vm = pl.BlockSpec(memory_space=pltpu.VMEM)
    dma = pltpu.SemaphoreType.DMA
    return pl.pallas_call(
        gather_parts,
        out_shape=jax.ShapeDtypeStruct((RUN, NH * HD), F32),
        in_specs=[vm, vm],
        out_specs=vm,
        scratch_shapes=[
            pltpu.VMEM((NY, NH, RUN, HD), jnp.int16), pltpu.VMEM((NY, NH, 8, RUN), F32), pltpu.VMEM((NH, RUN, HD), F32),
            dma, dma((NH,)), dma((NY, NX)), dma((NY, NX)), dma, dma,
        ],
        compiler_params=pltpu.CompilerParams(collective_id=2, has_side_effects=True, vmem_limit_bytes=8 << 20),
        name="gather_parts",
    )(parts, stats)


def on_device(queries, keys, values, positions):
    q, k, v = spread_call(queries, keys, values)
    return gather_call(*attend_call(positions.reshape(-1, RUN), q, k, v, GROUP, REACH))


def solution(mesh):
    finer = Mesh(mesh.devices.reshape(2, NX, NC, 2, NZ), AXES)
    placed = (P(AXES, None), P(AXES, None), P(AXES, None), P())
    return jax.shard_map(on_device, mesh=finer, in_specs=placed, out_specs=P(AXES, None), check_vma=False)
```

```python
import functools

import jax
import jax.numpy as jnp
from jax import lax
from jax.experimental import pallas as pl
from jax.experimental.pallas import tpu as pltpu
from jax.sharding import Mesh
from jax.sharding import PartitionSpec as P

AXES = ("yh", "x", "c", "yl", "z")
NX, NC, NY, NZ = 4, 2, 4, 8
NH = NX * NC
HD = 128
RUN = 128
C = 1.4426950408889634 / HD**0.5
F32, BF16 = jnp.float32, jnp.bfloat16
GROUP, REACH = 4, 8
NT = (((1,), (1,)), ((), ()))
LOW, HIGH = 2.0**-60, 2.0**100
EMPTY = -1e30
STEPS, TINY = 32767.0, 2.0**-110

def plan(pos_ref, meta, n_q):
    x, c, y, z = here()
    n = pos_ref.shape[0]
    first = pos_ref[...].astype(F32) * (1.0 / RUN)
    column = first[:, :1]
    row = jnp.concatenate([first[i : i + RUN].T[:1] for i in range(0, n, RUN)], axis=1)

    def coords(axis, shape):
        i = lax.broadcasted_iota(jnp.int32, shape, axis)
        iz, iyl, ic, ix, iyh = i % NZ, i // NZ % 2, i // (2 * NZ) % NC, i // (2 * NZ * NC) % NX, i // (2 * NZ * NC * NX)
        iy = 2 * iyh + iyl
        return iz == z, iy == y, iy * NH + ix * NC + ic, (ix * NC + ic) * NZ + iz

    q_row, k_row, _, _ = coords(1, (1, n))
    q_col, k_col, q_slot, k_slot = coords(0, (n, 1))
    below = row < column

    def count(mask):
        return jnp.sum(jnp.where(mask, 1.0, 0.0), axis=1, keepdims=True)

    spot = lax.broadcasted_iota(jnp.int32, (1, RUN), 1).astype(F32)

    def sorted_by_rank(here_col, here_row, things):
        place = count(jnp.logical_and(below, here_row))
        hit = jnp.logical_and(place == spot, here_col)
        return [jnp.sum(jnp.where(hit, thing, 0.0), axis=0, keepdims=True) for thing in things]

    seen = count(jnp.logical_and(row <= column, k_row))
    order, held, sees = sorted_by_rank(q_col, q_row, (q_slot.astype(F32), column, seen))
    held = jnp.where(spot < n_q, held, -1.0)
    rows = [order, held, sees] + sorted_by_rank(k_col, k_row, (k_slot.astype(F32), column))
    meta[...] = jnp.concatenate(rows + [jnp.zeros((3, RUN), F32)], axis=0).astype(jnp.int32)


def attend(group, reach, n_q, n_k, pos_ref, q_ref, k_ref, v_ref, out_ref, stat_ref, s0, s1, acc, sums, found, meta, sem):
    blocks = n_q // group
    plan(pos_ref, found, n_q)
    copy = pltpu.make_async_copy(found, meta, sem)
    copy.start()
    copy.wait()

    def chunks(b):
        top = meta[2, jnp.minimum(b * group + group - 1, n_q - 1)]
        return jnp.where(b < blocks, jnp.maximum((top + reach - 1) // reach, 1), 1)

    diff = lax.broadcasted_iota(jnp.int32, (RUN, RUN), 1) - lax.broadcasted_iota(jnp.int32, (RUN, RUN), 0)

    def rows_q(b):
        return jnp.concatenate([q_ref[meta[0, b * group + g]] for g in range(group)], axis=0)

    def rows_k(ref, j):
        return jnp.concatenate([ref[meta[3, j * reach + r]] for r in range(reach)], axis=0)

    def scores(b, j, s_ref):
        s_ref[...] = lax.dot_general(rows_q(b), rows_k(k_ref, j), NT, preferred_element_type=F32)

    def weigh(b, j, s_ref):
        both, part = [], []
        for g in range(group):
            own = meta[1, b * group + g]
            row_h, row_l, row_s = [], [], None
            for r in range(reach):
                gap = (own - meta[4, j * reach + r]) * RUN
                s = s_ref[g * RUN : (g + 1) * RUN, r * RUN : (r + 1) * RUN]
                p = jnp.where(diff <= gap, jnp.exp2(s * C), 0.0)
                h = p.astype(BF16)
                row_h.append(h)
                row_l.append((p - h.astype(F32)).astype(BF16))
                row_s = p if row_s is None else row_s + p
            both.append(jnp.concatenate([x for pair in zip(row_h, row_l) for x in pair], axis=1))
            part.append(row_s)
        twice = jnp.concatenate([v_ref[meta[3, j * reach + r]] for r in range(reach) for _ in range(2)], axis=0)
        new = jnp.dot(jnp.concatenate(both, axis=0), twice, preferred_element_type=F32)
        at = pl.ds(pl.multiple_of(b * group * RUN, RUN), group * RUN)
        first = j == 0
        acc[at, :] = jnp.where(first, 0.0, acc[at, :]) + new
        sums[at, :] = jnp.where(first, 0.0, sums[at, :]) + jnp.concatenate(part, axis=0)

    def after(b, j):
        b = jnp.minimum(b, blocks)
        last = j + 1 >= chunks(b)
        return jnp.minimum(jnp.where(last, b + 1, b), blocks), jnp.where(last, 0, j + 1)

    total_chunks = functools.reduce(jnp.add, [chunks(b) for b in range(blocks)])
    scores(0, 0, s0)

    def pair(_, at):
        b, j = at
        b1, j1 = after(b, j)
        weigh(b, j, s0)
        scores(b1, j1, s1)
        b2, j2 = after(b1, j1)
        weigh(b1, j1, s1)
        scores(b2, j2, s0)
        return b2, j2

    lax.fori_loop(0, (total_chunks + 1) // 2, pair, (jnp.int32(0), jnp.int32(0)))

    lanes = lax.broadcasted_iota(jnp.int32, (RUN, RUN), 1)

    def coded(got, total):
        mean = got * jnp.where(total > 0.0, 1.0 / total, 0.0)
        reach_of = jnp.maximum(jnp.max(jnp.abs(mean), axis=1, keepdims=True), TINY)
        return jnp.round(mean * (STEPS / reach_of)).astype(jnp.int32).astype(jnp.int16), reach_of

    def close(p, table):
        at = pl.ds(pl.multiple_of(p * RUN, RUN), RUN)
        total = jnp.sum(sums[at, :], axis=1, keepdims=True)
        out_ref[meta[0, p]], widest = coded(acc[at, :], total)
        return jnp.where(lanes == 2 * p, total, jnp.where(lanes == 2 * p + 1, widest, table))

    table = lax.fori_loop(0, n_q, close, jnp.zeros((RUN, RUN), F32), unroll=4).T
    outside = jnp.zeros((1, RUN), F32)
    for p in range(n_q):
        seen = meta[2, p] > 0
        total = table[2 * p : 2 * p + 1]
        good = jnp.logical_and(total > LOW, total < HIGH)
        outside += jnp.where(good, 0.0, jnp.where(seen, 1.0, 0.0))
        peak = jnp.full((6, RUN), jnp.where(seen, 0.0, EMPTY), F32)
        stat_ref[meta[0, p]] = jnp.concatenate([table[2 * p : 2 * p + 2], peak], axis=0)

    @pl.when(jnp.sum(outside) > 0.0)
    def _():
        def again(p, _):
            slot = meta[0, p]
            q = q_ref[slot]
            own = meta[1, p]

            def step(i, state):
                top, tot, got = state
                run = meta[3, i]
                gap = (own - meta[4, i]) * RUN
                s = lax.dot_general(q, k_ref[run], NT, preferred_element_type=F32) * C
                keep = diff <= gap
                s = jnp.where(keep, s, EMPTY)
                new = jnp.maximum(top, jnp.max(s, axis=1, keepdims=True))
                w = jnp.where(keep, jnp.exp2(s - new), 0.0)
                f = jnp.exp2(top - new)
                h = w.astype(BF16)
                l = (w - h.astype(F32)).astype(BF16)
                v = v_ref[run]
                got = got * f + (jnp.dot(h, v, preferred_element_type=F32) + jnp.dot(l, v, preferred_element_type=F32))
                return new, tot * f + jnp.sum(w, axis=1, keepdims=True), got

            zero = jnp.zeros((RUN, 1), F32)
            top, tot, got = lax.fori_loop(0, meta[2, p], step, (zero + EMPTY, zero, jnp.zeros((RUN, HD), F32)))
            out_ref[slot], widest = coded(got, tot)
            stat_ref[slot] = jnp.where(lanes == 0, tot, jnp.where(lanes == 1, widest, top)).T[:8]
            return 0

        lax.fori_loop(0, n_q, again, 0)


def attend_call(first, q, k, v, group, reach):
    n_q, n_k = q.shape[0], k.shape[0]
    vm = pl.BlockSpec(memory_space=pltpu.VMEM)
    return pl.pallas_call(
        functools.partial(attend, group, reach, n_q, n_k),
        out_shape=(
            jax.ShapeDtypeStruct((n_q, RUN, HD), jnp.int16),
            jax.ShapeDtypeStruct((n_q, 8, RUN), F32),
        ),
        in_specs=[vm, vm, vm, vm],
        out_specs=(vm, vm),
        scratch_shapes=[
            pltpu.VMEM((group * RUN, reach * RUN), F32),
            pltpu.VMEM((group * RUN, reach * RUN), F32),
            pltpu.VMEM(((n_q + group) * RUN, HD), F32),
            pltpu.VMEM(((n_q + group) * RUN, RUN), F32),
            pltpu.VMEM((8, RUN), jnp.int32),
            pltpu.SMEM((8, RUN), jnp.int32),
            pltpu.SemaphoreType.DMA,
        ],
        compiler_params=pltpu.CompilerParams(vmem_limit_bytes=20 << 20),
        name="attend",
    )(first, q, k, v)


def here():
    y = lax.axis_index("yh") * 2 + lax.axis_index("yl")
    return lax.axis_index("x"), lax.axis_index("c"), y, lax.axis_index("z")


def device(x, c, y, z):
    return {"yh": y // 2, "x": x, "c": c, "yl": y % 2, "z": z}


def remote(src, dst, send_sem, recv_sem, target):
    return pltpu.make_async_remote_copy(
        src_ref=src, dst_ref=dst, send_sem=send_sem, recv_sem=recv_sem,
        device_id=device(*target), device_id_type=pl.DeviceIdType.MESH,
    )


def spread(all_ref, qo, ko, vo, q_in, k_in, v_in, kc_in, vc_in, q_near, q_far, k_z, k_x, v_x, v_z, k_c, v_c):
    x, c, y, z = here()
    lane = x * NC + c
    k_ref, v_ref = all_ref.at[:, pl.ds(NH * HD, HD)], all_ref.at[:, pl.ds((NH + 1) * HD, HD)]

    barrier = pltpu.get_barrier_semaphore()

    def greet(*where):
        pl.semaphore_signal(barrier, 1, device_id=device(*where), device_id_type=pl.DeviceIdType.MESH)

    for d in (1, NZ - 1):
        greet(x, c, y, (z + d) % NZ)
    for d in range(1, NH):
        to = (lane + d) % NH
        greet(to // NC, to % NC, y, z)
    for d in range(1, NY):
        greet(x, c, (y + d) % NY, z)
    pl.semaphore_wait(barrier, NH + NY)

    def go(copy):
        copy.start()

    def at_x(d):
        return (x + d) % NX

    def at_z(d):
        return (z + d) % NZ

    def slot(dx, dz):
        return (at_x(dx) * NC + c) * NZ + at_z(dz)

    def k_to_x(dz, d):
        s = slot(0, dz)
        go(remote(ko.at[s], ko.at[s], k_x, k_in.at[x, at_z(dz)], (at_x(d), c, y, z)))

    def v_to_z(dx, dz, d):
        s = slot(dx, dz)
        go(remote(vo.at[s], vo.at[s], v_z, v_in.at[at_x(dx), at_z(dz)], (x, c, y, at_z(d))))

    def share(dx, dz, ref, out, into):
        s = slot(dx, dz)
        go(remote(ref.at[s], ref.at[s], out, into, (x, 1 - c, y, z)))

    def got(ref, s, sem):
        pltpu.make_async_copy(ref.at[s], ref.at[s], sem).wait()

    def got_k(dx, dz):
        got(ko, slot(dx, dz), k_in.at[at_x(dx), at_z(dz)])

    def got_v(dx, dz):
        got(vo, slot(dx, dz), v_in.at[at_x(dx), at_z(dz)])

    def got_q(d, h):
        yy = (y + d) % NY
        got(qo, yy * NH + h, q_in.at[yy, h])

    def q_cols(h):
        return all_ref.at[:, pl.ds(pl.multiple_of(h * HD, HD), HD)]

    own_q, own = qo.at[y * NH + lane], slot(0, 0)
    for d in (1, 3, 2):
        go(remote(v_ref, vo.at[own], v_x, v_in.at[x, z], (at_x(d), c, y, z)))
    for d in (1, -1):
        go(remote(k_ref, ko.at[own], k_z, k_in.at[x, z], (x, c, y, at_z(d))))
    for d in range(1, NH):
        to = (lane + d) % NH
        go(remote(q_cols(to), own_q, q_near, q_in.at[y, lane], (to // NC, to % NC, y, z)))
    pltpu.make_async_copy(k_ref, ko.at[own], k_in.at[x, z]).start()
    pltpu.make_async_copy(v_ref, vo.at[own], v_in.at[x, z]).start()
    pltpu.make_async_copy(q_cols(lane), own_q, q_in.at[y, lane]).start()

    def side(t):
        d = (t + 1) // 2
        return d if t % 2 else -d

    def k_step(t):
        dz = -side(t)
        s = slot(0, dz)
        got_k(0, dz)
        if -NZ // 2 < dz < 0:
            go(remote(ko.at[s], ko.at[s], k_z, k_in.at[x, at_z(dz)], (x, c, y, at_z(1))))
        elif 0 < dz < NZ // 2 - 1:
            go(remote(ko.at[s], ko.at[s], k_z, k_in.at[x, at_z(dz)], (x, c, y, at_z(-1))))
        for d in (1, 3, 2):
            k_to_x(dz, d)
        share(0, dz, ko, k_c, kc_in)

    def k_rest(t):
        for dx in (1, -1, 2):
            got_k(dx, -side(t))
            share(dx, -side(t), ko, k_c, kc_in)

    def v_start(dx):
        got_v(dx, 0)
        v_to_z(dx, 0, 1)
        v_to_z(dx, 0, -1)
        share(dx, 0, vo, v_c, vc_in)

    def v_step(t):
        dz = side(t)
        for dx in (0, 1, -1, 2):
            got_v(dx, dz)
            if 0 < dz < NZ // 2:
                v_to_z(dx, dz, -1)
            elif 1 - NZ // 2 < dz < 0:
                v_to_z(dx, dz, 1)
            share(dx, dz, vo, v_c, vc_in)

    def q_step(t):
        h = (lane + t) % NH
        s = y * NH + h
        got_q(0, h)
        for d in (1, 3, 2):
            go(remote(qo.at[s], qo.at[s], q_far, q_in.at[y, h], (x, c, (y + d) % NY, z)))

    def near(t):
        k_step(t)
        q_step(t)

    v_start(0)
    near(0)
    for dx in (1, -1, 2):
        v_start(dx)
    near(1)
    v_step(1)
    v_step(2)
    near(2)
    near(3)
    v_step(3)
    v_step(4)
    near(4)
    near(5)
    k_rest(0)
    k_rest(1)
    v_step(5)
    v_step(6)
    near(6)
    near(7)
    k_rest(2)
    k_rest(3)
    v_step(7)
    for t in (4, 5, 6, 7):
        k_rest(t)

    def q_rest(i, _):
        got_q(1 + i // NH, i % NH)
        return 0

    lax.fori_loop(0, (NY - 1) * NH, q_rest, 0)
    for sem, count in (
        (kc_in, 32), (vc_in, 32), (q_near, 7), (q_far, 24), (k_z, 7), (k_x, 24), (v_x, 3), (v_z, 28), (k_c, 32), (v_c, 32),
    ):
        some = pl.ds(0, count)
        got(ko, some, sem)


def spread_call(together):
    vm = pl.BlockSpec(memory_space=pltpu.VMEM)
    held = pl.BlockSpec(memory_space=pl.ANY)
    dma = pltpu.SemaphoreType.DMA
    grid = (NX, NZ)
    return pl.pallas_call(
        spread,
        out_shape=(
            jax.ShapeDtypeStruct((NY * NH, RUN, HD), BF16),
            jax.ShapeDtypeStruct((NH * NZ, RUN, HD), BF16),
            jax.ShapeDtypeStruct((NH * NZ, RUN, HD), BF16),
        ),
        in_specs=[held],
        out_specs=(vm, vm, vm),
        scratch_shapes=[
            dma((NY, NH)), dma(grid), dma(grid), dma, dma, dma, dma, dma, dma, dma, dma, dma, dma,
        ],
        compiler_params=pltpu.CompilerParams(collective_id=1, has_side_effects=True, vmem_limit_bytes=8 << 20),
        name="spread",
    )(together)


def gather_parts(p_ref, t_ref, o_ref, got, stat, merged, far, near_in, p_in, t_in, p_out, t_out):
    x, c, y, z = here()
    lane = x * NC + c
    mine = pl.ds(pl.multiple_of(lane * HD, HD), HD)

    barrier = pltpu.get_barrier_semaphore()

    def greet(*where):
        pl.semaphore_signal(barrier, 1, device_id=device(*where), device_id_type=pl.DeviceIdType.MESH)

    for d in range(1, NY):
        greet(x, c, (y + d) % NY, z)
    for d in range(1, NH):
        to = (lane + d) % NH
        greet(to // NC, to % NC, y, z)
    pl.semaphore_wait(barrier, NY + NH - 2)

    order = (1, 3, 2, 0)
    for dx in order:
        xx = (x + dx) % NX
        for d in (1, 3, 2):
            yy = (y + d) % NY
            here_ = pl.ds(yy * NH + xx * NC, NC)
            lands = pl.ds(xx * NC, NC)
            remote(p_ref.at[here_], got.at[NY - d, lands], p_out, p_in.at[NY - d, xx], (x, c, yy, z)).start()
            remote(t_ref.at[here_], stat.at[NY - d, lands], t_out, t_in.at[NY - d, xx], (x, c, yy, z)).start()

    for dx in order:
        xx = (x + dx) % NX
        lands = pl.ds(xx * NC, NC)
        for d in (1, 3, 2):
            pltpu.make_async_copy(got.at[d, lands], got.at[d, lands], p_in.at[d, xx]).wait()
            pltpu.make_async_copy(stat.at[d, lands], stat.at[d, lands], t_in.at[d, xx]).wait()
        rows = []
        for cc in range(NC):
            to = xx * NC + cc
            stats = [t_ref[y * NH + to]] + [stat[d, to] for d in range(1, NY)]
            top = functools.reduce(jnp.maximum, [s[2:3] for s in stats])
            shares = [jnp.exp2(s[2:3] - top) * s[0:1] for s in stats]
            whole = functools.reduce(jnp.add, shares)
            rows += [f / whole * (s[1:2] * (1.0 / STEPS)) for f, s in zip(shares, stats)]
        weights = jnp.concatenate(rows + [jnp.zeros((RUN - NC * NY, RUN), F32)], axis=0).T
        for cc in range(NC):
            to = xx * NC + cc
            parts = [p_ref[y * NH + to]] + [got[d, to] for d in range(1, NY)]
            merged[to] = functools.reduce(
                jnp.add,
                [p.astype(jnp.int32).astype(F32) * weights[:, cc * NY + i : cc * NY + i + 1] for i, p in enumerate(parts)],
            )

            def send(to=to, cc=cc):
                remote(merged.at[to], o_ref.at[:, mine], far, near_in.at[lane], (xx, cc, y, z)).start()

            if dx:
                send()
            else:
                pl.when(c != cc)(send)

    o_ref[:, mine] = merged[lane]

    def landed(i, _):
        h = (lane + i) % NH
        cols = o_ref.at[:, pl.ds(pl.multiple_of(h * HD, HD), HD)]
        pltpu.make_async_copy(cols, cols, near_in.at[h]).wait()
        return 0

    lax.fori_loop(1, NH, landed, 0)
    sent = merged.at[pl.ds(0, NH - 1)]
    pltpu.make_async_copy(sent, sent, far).wait()
    for ref, sem in ((p_ref, p_out), (t_ref, t_out)):
        sent = ref.at[pl.ds(0, (NY - 1) * NH)]
        pltpu.make_async_copy(sent, sent, sem).wait()


def gather_call(parts, stats):
    vm = pl.BlockSpec(memory_space=pltpu.VMEM)
    dma = pltpu.SemaphoreType.DMA
    return pl.pallas_call(
        gather_parts,
        out_shape=jax.ShapeDtypeStruct((RUN, NH * HD), F32),
        in_specs=[vm, vm],
        out_specs=vm,
        scratch_shapes=[
            pltpu.VMEM((NY, NH, RUN, HD), jnp.int16), pltpu.VMEM((NY, NH, 8, RUN), F32), pltpu.VMEM((NH, RUN, HD), F32),
            dma, dma((NH,)), dma((NY, NX)), dma((NY, NX)), dma, dma,
        ],
        compiler_params=pltpu.CompilerParams(collective_id=2, has_side_effects=True, vmem_limit_bytes=8 << 20),
        name="gather_parts",
    )(parts, stats)


def on_device(queries, keys, values, positions):
    q, k, v = spread_call(jnp.concatenate([queries, keys, values], axis=1))
    return gather_call(*attend_call(positions.reshape(-1, RUN), q, k, v, GROUP, REACH))


def solution(mesh):
    finer = Mesh(mesh.devices.reshape(2, NX, NC, 2, NZ), AXES)
    placed = (P(AXES, None), P(AXES, None), P(AXES, None), P())
    return jax.shard_map(on_device, mesh=finer, in_specs=placed, out_specs=P(AXES, None), check_vma=False)
```

```python
import functools

import jax
import jax.numpy as jnp
from jax import lax
from jax.experimental import pallas as pl
from jax.experimental.pallas import tpu as pltpu
from jax.sharding import Mesh
from jax.sharding import PartitionSpec as P

AXES = ("yh", "x", "c", "yl", "z")
NX, NC, NY, NZ = 4, 2, 4, 8
NH = NX * NC
HD = 128
RUN = 128
C = 1.4426950408889634 / HD**0.5
F32, BF16 = jnp.float32, jnp.bfloat16
GROUP, REACH = 4, 8
NT = (((1,), (1,)), ((), ()))
LOW, HIGH = 2.0**-60, 2.0**100
EMPTY = -1e30
STEPS, TINY = 32767.0, 2.0**-110

def plan(pos_ref, meta, n_q):
    x, c, y, z = here()
    n = pos_ref.shape[0]
    first = pos_ref[...].astype(F32) * (1.0 / RUN)
    column = first[:, :1]
    row = jnp.concatenate([first[i : i + RUN].T[:1] for i in range(0, n, RUN)], axis=1)

    def coords(axis, shape):
        i = lax.broadcasted_iota(jnp.int32, shape, axis)
        iz, iyl, ic, ix, iyh = i % NZ, i // NZ % 2, i // (2 * NZ) % NC, i // (2 * NZ * NC) % NX, i // (2 * NZ * NC * NX)
        iy = 2 * iyh + iyl
        return iz == z, iy == y, iy * NH + ix * NC + ic, (ix * NC + ic) * NZ + iz

    q_row, k_row, _, _ = coords(1, (1, n))
    q_col, k_col, q_slot, k_slot = coords(0, (n, 1))
    below = row < column

    def count(mask):
        return jnp.sum(jnp.where(mask, 1.0, 0.0), axis=1, keepdims=True)

    spot = lax.broadcasted_iota(jnp.int32, (1, RUN), 1).astype(F32)

    def sorted_by_rank(here_col, here_row, things):
        place = count(jnp.logical_and(below, here_row))
        hit = jnp.logical_and(place == spot, here_col)
        return [jnp.sum(jnp.where(hit, thing, 0.0), axis=0, keepdims=True) for thing in things]

    seen = count(jnp.logical_and(row <= column, k_row))
    order, held, sees = sorted_by_rank(q_col, q_row, (q_slot.astype(F32), column, seen))
    held = jnp.where(spot < n_q, held, -1.0)
    rows = [order, held, sees] + sorted_by_rank(k_col, k_row, (k_slot.astype(F32), column))
    meta[...] = jnp.concatenate(rows + [jnp.zeros((3, RUN), F32)], axis=0).astype(jnp.int32)


def attend(group, reach, n_q, n_k, pos_ref, q_ref, k_ref, v_ref, out_ref, stat_ref, s0, s1, acc, sums, found, meta, sem):
    blocks = n_q // group
    plan(pos_ref, found, n_q)
    copy = pltpu.make_async_copy(found, meta, sem)
    copy.start()
    copy.wait()

    def chunks(b):
        top = meta[2, jnp.minimum(b * group + group - 1, n_q - 1)]
        return jnp.where(b < blocks, jnp.maximum((top + reach - 1) // reach, 1), 1)

    diff = lax.broadcasted_iota(jnp.int32, (RUN, RUN), 1) - lax.broadcasted_iota(jnp.int32, (RUN, RUN), 0)

    def rows_q(b):
        return jnp.concatenate([q_ref[meta[0, b * group + g]] for g in range(group)], axis=0)

    def rows_k(ref, j):
        return jnp.concatenate([ref[meta[3, j * reach + r]] for r in range(reach)], axis=0)

    def scores(b, j, s_ref):
        s_ref[...] = lax.dot_general(rows_q(b), rows_k(k_ref, j), NT, preferred_element_type=F32)

    def weigh(b, j, s_ref):
        both, part = [], []
        for g in range(group):
            own = meta[1, b * group + g]
            row_h, row_l, row_s = [], [], None
            for r in range(reach):
                gap = (own - meta[4, j * reach + r]) * RUN
                s = s_ref[g * RUN : (g + 1) * RUN, r * RUN : (r + 1) * RUN]
                p = jnp.where(diff <= gap, jnp.exp2(s * C), 0.0)
                h = p.astype(BF16)
                row_h.append(h)
                row_l.append((p - h.astype(F32)).astype(BF16))
                row_s = p if row_s is None else row_s + p
            both.append(jnp.concatenate([x for pair in zip(row_h, row_l) for x in pair], axis=1))
            part.append(row_s)
        twice = jnp.concatenate([v_ref[meta[3, j * reach + r]] for r in range(reach) for _ in range(2)], axis=0)
        new = jnp.dot(jnp.concatenate(both, axis=0), twice, preferred_element_type=F32)
        at = pl.ds(pl.multiple_of(b * group * RUN, RUN), group * RUN)
        first = j == 0
        acc[at, :] = jnp.where(first, 0.0, acc[at, :]) + new
        sums[at, :] = jnp.where(first, 0.0, sums[at, :]) + jnp.concatenate(part, axis=0)

    def after(b, j):
        b = jnp.minimum(b, blocks)
        last = j + 1 >= chunks(b)
        return jnp.minimum(jnp.where(last, b + 1, b), blocks), jnp.where(last, 0, j + 1)

    total_chunks = functools.reduce(jnp.add, [chunks(b) for b in range(blocks)])
    scores(0, 0, s0)

    def pair(_, at):
        b, j = at
        b1, j1 = after(b, j)
        weigh(b, j, s0)
        scores(b1, j1, s1)
        b2, j2 = after(b1, j1)
        weigh(b1, j1, s1)
        scores(b2, j2, s0)
        return b2, j2

    lax.fori_loop(0, (total_chunks + 1) // 2, pair, (jnp.int32(0), jnp.int32(0)))

    lanes = lax.broadcasted_iota(jnp.int32, (RUN, RUN), 1)

    def coded(got, total):
        mean = got * jnp.where(total > 0.0, 1.0 / total, 0.0)
        reach_of = jnp.maximum(jnp.max(jnp.abs(mean), axis=1, keepdims=True), TINY)
        return jnp.round(mean * (STEPS / reach_of)).astype(jnp.int32).astype(jnp.int16), reach_of

    def close(p, table):
        at = pl.ds(pl.multiple_of(p * RUN, RUN), RUN)
        total = jnp.sum(sums[at, :], axis=1, keepdims=True)
        out_ref[meta[0, p]], widest = coded(acc[at, :], total)
        return jnp.where(lanes == 2 * p, total, jnp.where(lanes == 2 * p + 1, widest, table))

    table = lax.fori_loop(0, n_q, close, jnp.zeros((RUN, RUN), F32), unroll=4).T
    outside = jnp.zeros((1, RUN), F32)
    for p in range(n_q):
        seen = meta[2, p] > 0
        total = table[2 * p : 2 * p + 1]
        good = jnp.logical_and(total > LOW, total < HIGH)
        outside += jnp.where(good, 0.0, jnp.where(seen, 1.0, 0.0))
        peak = jnp.full((2, RUN), jnp.where(seen, 0.0, EMPTY), F32)
        stat_ref[meta[0, p]] = jnp.concatenate([table[2 * p : 2 * p + 2], peak], axis=0)

    @pl.when(jnp.sum(outside) > 0.0)
    def _():
        def again(p, _):
            slot = meta[0, p]
            q = q_ref[slot]
            own = meta[1, p]

            def step(i, state):
                top, tot, got = state
                run = meta[3, i]
                gap = (own - meta[4, i]) * RUN
                s = lax.dot_general(q, k_ref[run], NT, preferred_element_type=F32) * C
                keep = diff <= gap
                s = jnp.where(keep, s, EMPTY)
                new = jnp.maximum(top, jnp.max(s, axis=1, keepdims=True))
                w = jnp.where(keep, jnp.exp2(s - new), 0.0)
                f = jnp.exp2(top - new)
                h = w.astype(BF16)
                l = (w - h.astype(F32)).astype(BF16)
                v = v_ref[run]
                got = got * f + (jnp.dot(h, v, preferred_element_type=F32) + jnp.dot(l, v, preferred_element_type=F32))
                return new, tot * f + jnp.sum(w, axis=1, keepdims=True), got

            zero = jnp.zeros((RUN, 1), F32)
            top, tot, got = lax.fori_loop(0, meta[2, p], step, (zero + EMPTY, zero, jnp.zeros((RUN, HD), F32)))
            out_ref[slot], widest = coded(got, tot)
            stat_ref[slot] = jnp.where(lanes == 0, tot, jnp.where(lanes == 1, widest, top)).T[:4]
            return 0

        lax.fori_loop(0, n_q, again, 0)


def attend_call(first, q, k, v, group, reach):
    n_q, n_k = q.shape[0], k.shape[0]
    vm = pl.BlockSpec(memory_space=pltpu.VMEM)
    return pl.pallas_call(
        functools.partial(attend, group, reach, n_q, n_k),
        out_shape=(
            jax.ShapeDtypeStruct((n_q, RUN, HD), jnp.int16),
            jax.ShapeDtypeStruct((n_q, 4, RUN), F32),
        ),
        in_specs=[vm, vm, vm, vm],
        out_specs=(vm, vm),
        scratch_shapes=[
            pltpu.VMEM((group * RUN, reach * RUN), F32),
            pltpu.VMEM((group * RUN, reach * RUN), F32),
            pltpu.VMEM(((n_q + group) * RUN, HD), F32),
            pltpu.VMEM(((n_q + group) * RUN, RUN), F32),
            pltpu.VMEM((8, RUN), jnp.int32),
            pltpu.SMEM((8, RUN), jnp.int32),
            pltpu.SemaphoreType.DMA,
        ],
        compiler_params=pltpu.CompilerParams(vmem_limit_bytes=20 << 20),
        name="attend",
    )(first, q, k, v)


def here():
    y = lax.axis_index("yh") * 2 + lax.axis_index("yl")
    return lax.axis_index("x"), lax.axis_index("c"), y, lax.axis_index("z")


def device(x, c, y, z):
    return {"yh": y // 2, "x": x, "c": c, "yl": y % 2, "z": z}


def remote(src, dst, send_sem, recv_sem, target):
    return pltpu.make_async_remote_copy(
        src_ref=src, dst_ref=dst, send_sem=send_sem, recv_sem=recv_sem,
        device_id=device(*target), device_id_type=pl.DeviceIdType.MESH,
    )


def spread(all_ref, qo, ko, vo, q_in, k_in, v_in, kc_in, vc_in, q_near, q_far, k_z, k_x, v_x, v_z, k_c, v_c):
    x, c, y, z = here()
    lane = x * NC + c
    k_ref, v_ref = all_ref.at[:, pl.ds(NH * HD, HD)], all_ref.at[:, pl.ds((NH + 1) * HD, HD)]

    def q_cols(h):
        return all_ref.at[:, pl.ds(pl.multiple_of(h * HD, HD), HD)]

    own_q, own = qo.at[y * NH + lane], lane * NZ + z
    pltpu.make_async_copy(k_ref, ko.at[own], k_in.at[x, z]).start()
    pltpu.make_async_copy(v_ref, vo.at[own], v_in.at[x, z]).start()
    pltpu.make_async_copy(q_cols(lane), own_q, q_in.at[y, lane]).start()

    barrier = pltpu.get_barrier_semaphore()

    def greet(*where):
        pl.semaphore_signal(barrier, 1, device_id=device(*where), device_id_type=pl.DeviceIdType.MESH)

    for d in (1, NZ - 1):
        greet(x, c, y, (z + d) % NZ)
    for d in range(1, NH):
        to = (lane + d) % NH
        greet(to // NC, to % NC, y, z)
    for d in range(1, NY):
        greet(x, c, (y + d) % NY, z)
    pl.semaphore_wait(barrier, NH + NY)

    def go(copy):
        copy.start()

    def at_x(d):
        return (x + d) % NX

    def at_z(d):
        return (z + d) % NZ

    def slot(dx, dz):
        return (at_x(dx) * NC + c) * NZ + at_z(dz)

    def k_to_x(dz, d):
        s = slot(0, dz)
        go(remote(ko.at[s], ko.at[s], k_x, k_in.at[x, at_z(dz)], (at_x(d), c, y, z)))

    def v_to_z(dx, dz, d):
        s = slot(dx, dz)
        go(remote(vo.at[s], vo.at[s], v_z, v_in.at[at_x(dx), at_z(dz)], (x, c, y, at_z(d))))

    def share(dx, dz, ref, out, into):
        s = slot(dx, dz)
        go(remote(ref.at[s], ref.at[s], out, into, (x, 1 - c, y, z)))

    def got(ref, s, sem):
        pltpu.make_async_copy(ref.at[s], ref.at[s], sem).wait()

    def got_k(dx, dz):
        got(ko, slot(dx, dz), k_in.at[at_x(dx), at_z(dz)])

    def got_v(dx, dz):
        got(vo, slot(dx, dz), v_in.at[at_x(dx), at_z(dz)])

    def got_q(d, h):
        yy = (y + d) % NY
        got(qo, yy * NH + h, q_in.at[yy, h])

    for d in (1, 3, 2):
        go(remote(v_ref, vo.at[own], v_x, v_in.at[x, z], (at_x(d), c, y, z)))
    for d in (1, -1):
        go(remote(k_ref, ko.at[own], k_z, k_in.at[x, z], (x, c, y, at_z(d))))
    for d in range(1, NH):
        to = (lane + d) % NH
        go(remote(q_cols(to), own_q, q_near, q_in.at[y, lane], (to // NC, to % NC, y, z)))

    def side(t):
        d = (t + 1) // 2
        return d if t % 2 else -d

    def k_step(t):
        dz = -side(t)
        s = slot(0, dz)
        got_k(0, dz)
        if -NZ // 2 < dz < 0:
            go(remote(ko.at[s], ko.at[s], k_z, k_in.at[x, at_z(dz)], (x, c, y, at_z(1))))
        elif 0 < dz < NZ // 2 - 1:
            go(remote(ko.at[s], ko.at[s], k_z, k_in.at[x, at_z(dz)], (x, c, y, at_z(-1))))
        for d in (1, 3, 2):
            k_to_x(dz, d)
        share(0, dz, ko, k_c, kc_in)

    def k_rest(t):
        for dx in (1, -1, 2):
            got_k(dx, -side(t))
            share(dx, -side(t), ko, k_c, kc_in)

    def v_start(dx):
        got_v(dx, 0)
        v_to_z(dx, 0, 1)
        v_to_z(dx, 0, -1)
        share(dx, 0, vo, v_c, vc_in)

    def v_step(t):
        dz = side(t)
        for dx in (0, 1, -1, 2):
            got_v(dx, dz)
            if 0 < dz < NZ // 2:
                v_to_z(dx, dz, -1)
            elif 1 - NZ // 2 < dz < 0:
                v_to_z(dx, dz, 1)
            share(dx, dz, vo, v_c, vc_in)

    def q_step(t):
        h = (lane + t) % NH
        s = y * NH + h
        got_q(0, h)
        for d in (1, 3, 2):
            go(remote(qo.at[s], qo.at[s], q_far, q_in.at[y, h], (x, c, (y + d) % NY, z)))

    def near(t):
        k_step(t)
        q_step(t)

    v_start(0)
    near(0)
    for dx in (1, -1, 2):
        v_start(dx)
    near(1)
    v_step(1)
    v_step(2)
    near(2)
    near(3)
    v_step(3)
    v_step(4)
    near(4)
    near(5)
    k_rest(0)
    k_rest(1)
    v_step(5)
    v_step(6)
    near(6)
    near(7)
    k_rest(2)
    k_rest(3)
    v_step(7)
    for t in (4, 5, 6, 7):
        k_rest(t)

    def q_rest(i, _):
        got_q(1 + i // NH, i % NH)
        return 0

    lax.fori_loop(0, (NY - 1) * NH, q_rest, 0)
    for sem, count in (
        (kc_in, 32), (vc_in, 32), (q_near, 7), (q_far, 24), (k_z, 7), (k_x, 24), (v_x, 3), (v_z, 28), (k_c, 32), (v_c, 32),
    ):
        some = pl.ds(0, count)
        got(ko, some, sem)


def spread_call(together):
    vm = pl.BlockSpec(memory_space=pltpu.VMEM)
    held = pl.BlockSpec(memory_space=pl.ANY)
    dma = pltpu.SemaphoreType.DMA
    grid = (NX, NZ)
    return pl.pallas_call(
        spread,
        out_shape=(
            jax.ShapeDtypeStruct((NY * NH, RUN, HD), BF16),
            jax.ShapeDtypeStruct((NH * NZ, RUN, HD), BF16),
            jax.ShapeDtypeStruct((NH * NZ, RUN, HD), BF16),
        ),
        in_specs=[held],
        out_specs=(vm, vm, vm),
        scratch_shapes=[
            dma((NY, NH)), dma(grid), dma(grid), dma, dma, dma, dma, dma, dma, dma, dma, dma, dma,
        ],
        compiler_params=pltpu.CompilerParams(collective_id=1, has_side_effects=True, vmem_limit_bytes=8 << 20),
        name="spread",
    )(together)


def gather_parts(p_ref, t_ref, o_ref, got, stat, merged, far, near_in, p_in, t_in, p_out, t_out):
    x, c, y, z = here()
    lane = x * NC + c
    mine = pl.ds(pl.multiple_of(lane * HD, HD), HD)

    barrier = pltpu.get_barrier_semaphore()

    def greet(*where):
        pl.semaphore_signal(barrier, 1, device_id=device(*where), device_id_type=pl.DeviceIdType.MESH)

    for d in range(1, NY):
        greet(x, c, (y + d) % NY, z)
    for d in range(1, NH):
        to = (lane + d) % NH
        greet(to // NC, to % NC, y, z)
    pl.semaphore_wait(barrier, NY + NH - 2)

    order = (1, 3, 2, 0)
    for dx in order:
        xx = (x + dx) % NX
        for d in (1, 3, 2):
            yy = (y + d) % NY
            here_ = pl.ds(yy * NH + xx * NC, NC)
            lands = pl.ds(xx * NC, NC)
            remote(p_ref.at[here_], got.at[NY - d, lands], p_out, p_in.at[NY - d, xx], (x, c, yy, z)).start()
            remote(t_ref.at[here_], stat.at[NY - d, lands], t_out, t_in.at[NY - d, xx], (x, c, yy, z)).start()

    for dx in order:
        xx = (x + dx) % NX
        lands = pl.ds(xx * NC, NC)
        for d in (1, 3, 2):
            pltpu.make_async_copy(got.at[d, lands], got.at[d, lands], p_in.at[d, xx]).wait()
            pltpu.make_async_copy(stat.at[d, lands], stat.at[d, lands], t_in.at[d, xx]).wait()
        rows = []
        for cc in range(NC):
            to = xx * NC + cc
            stats = [t_ref[y * NH + to]] + [stat[d, to] for d in range(1, NY)]
            top = functools.reduce(jnp.maximum, [s[2:3] for s in stats])
            shares = [jnp.exp2(s[2:3] - top) * s[0:1] for s in stats]
            whole = functools.reduce(jnp.add, shares)
            rows += [f / whole * (s[1:2] * (1.0 / STEPS)) for f, s in zip(shares, stats)]
        weights = jnp.concatenate(rows + [jnp.zeros((RUN - NC * NY, RUN), F32)], axis=0).T
        for cc in range(NC):
            to = xx * NC + cc
            parts = [p_ref[y * NH + to]] + [got[d, to] for d in range(1, NY)]
            merged[to] = functools.reduce(
                jnp.add,
                [p.astype(jnp.int32).astype(F32) * weights[:, cc * NY + i : cc * NY + i + 1] for i, p in enumerate(parts)],
            )

            def send(to=to, cc=cc):
                remote(merged.at[to], o_ref.at[:, mine], far, near_in.at[lane], (xx, cc, y, z)).start()

            if dx:
                send()
            else:
                pl.when(c != cc)(send)

    o_ref[:, mine] = merged[lane]

    def landed(i, _):
        h = (lane + i) % NH
        cols = o_ref.at[:, pl.ds(pl.multiple_of(h * HD, HD), HD)]
        pltpu.make_async_copy(cols, cols, near_in.at[h]).wait()
        return 0

    lax.fori_loop(1, NH, landed, 0)
    sent = merged.at[pl.ds(0, NH - 1)]
    pltpu.make_async_copy(sent, sent, far).wait()
    for ref, sem in ((p_ref, p_out), (t_ref, t_out)):
        sent = ref.at[pl.ds(0, (NY - 1) * NH)]
        pltpu.make_async_copy(sent, sent, sem).wait()


def gather_call(parts, stats):
    vm = pl.BlockSpec(memory_space=pltpu.VMEM)
    dma = pltpu.SemaphoreType.DMA
    return pl.pallas_call(
        gather_parts,
        out_shape=jax.ShapeDtypeStruct((RUN, NH * HD), F32),
        in_specs=[vm, vm],
        out_specs=vm,
        scratch_shapes=[
            pltpu.VMEM((NY, NH, RUN, HD), jnp.int16), pltpu.VMEM((NY, NH, 4, RUN), F32), pltpu.VMEM((NH, RUN, HD), F32),
            dma, dma((NH,)), dma((NY, NX)), dma((NY, NX)), dma, dma,
        ],
        compiler_params=pltpu.CompilerParams(collective_id=2, has_side_effects=True, vmem_limit_bytes=8 << 20),
        name="gather_parts",
    )(parts, stats)


def on_device(queries, keys, values, positions):
    q, k, v = spread_call(jnp.concatenate([queries, keys, values], axis=1))
    return gather_call(*attend_call(positions.reshape(-1, RUN), q, k, v, GROUP, REACH))


def solution(mesh):
    finer = Mesh(mesh.devices.reshape(2, NX, NC, 2, NZ), AXES)
    placed = (P(AXES, None), P(AXES, None), P(AXES, None), P())
    return jax.shard_map(on_device, mesh=finer, in_specs=placed, out_specs=P(AXES, None), check_vma=False)
```
